32 devices in a mesh: tile: 8 (over z, x), agg: 4 (over y, core).
Axes of the slice: x: 2, y: 2, z: 4, core: 2. Of those that a mesh axis runs over, the one named last changes fastest.
Arguments:
- right_side: float32 [65536, 256], P(('tile', 'agg')), may hold values from -8 to 8
- diag_tiles: float32 [512, 128, 128], P(('tile', 'agg')), may hold values from -1 to 2
- smoother: float32 [512, 128, 128], P(('tile', 'agg')), may hold values from 0 to 1
- coupling_tiles: float32 [1024, 128, 128], P(('tile', 'agg')), may hold values from -0.003125 to 0
- tile_rows: int32 [1024], P(('tile', 'agg')), may hold values from 0 to 15
- tile_cols: int32 [1024], P(('tile', 'agg')), may hold values from 0 to 15
- cross_end: int32 [8, 4, 3, 4, 32], P('tile', 'agg'), may hold values from 0 to 2047
- cross_count: int32 [8, 4, 3, 4], P('tile', 'agg'), may hold values from 0 to 32, as said below
- cross_weight: float32 [8, 4, 3, 4, 32], P('tile', 'agg'), may hold values from 0.1 to 0.3, as said below
- block_agg: int32 [512, 1], P(('tile', 'agg')), may hold values from 0 to 31
- coarse_inverse: float32 [32, 32], P(('tile', 'agg')), may hold values from -1 to 1
Outputs:
- solution: float32 [65536, 256], P(('tile', 'agg'))
The draws below stay inside these ranges and needn't reach their ends.
Inputs may be any that keep to these rules, and one draw needn't show every extreme that they name: cross_count[t, g, k, h] equals cross_count[t + k - 1, h, 2 - k, g]; it is zero where t + k - 1 lies outside 0..7 and where k = 1 and h = g; some pair of devices of one tile has exactly 32. cross_weight[t, g, k, h, s] equals cross_weight[t + k - 1, h, 2 - k, g, s] wherever both exist.
All inputs are finite; a program needn't handle non-finite values.
Results may differ from the reference program's by a relative error of at most 0.0001.
Values sent between devices are 32-bit elements; how exact they have to be, the bound alone decides.
A program may use at most 64 MiB of HBM per device.

```python
import math
import jax
import jax.numpy as jnp
from jax import lax

DATES = 256
BLK = 128
NB_DEV = 16
CAP = 32
SWEEPS = 2
TILES = 8
OWNERS = 4
PTS_DEV = 2048
NT_DEV = 32
POINTS = 65536
BLOCKS = 512
COUPLES = 1024
NAGG = 32


def view_grid():
    tile_index = jnp.arange(TILES, dtype=jnp.int32)[:, None, None, None]
    own_index = jnp.arange(OWNERS, dtype=jnp.int32)[None, :, None, None]
    side_index = jnp.arange(3, dtype=jnp.int32)[None, None, :, None]
    peer_index = jnp.arange(OWNERS, dtype=jnp.int32)[None, None, None, :]
    return (tile_index, own_index, side_index, peer_index)


def mirror_view_drawn(values):
    tile_index, own_index, side_index, peer_index = view_grid()
    source_tile = jnp.clip(tile_index + side_index - 1, 0, TILES - 1)
    return values[source_tile, peer_index, 2 - side_index, own_index]


def view_masks():
    tile_index, own_index, side_index, peer_index = view_grid()
    canonical = (side_index == 2) | (side_index == 1) & (own_index < peer_index)
    neighbour = tile_index + side_index - 1
    valid_view = (neighbour >= 0) & (neighbour < TILES) & jnp.logical_not((side_index == 1) & (own_index == peer_index))
    return (canonical, valid_view)


def draw_cross_count(key, part):
    base_key = jax.random.fold_in(key, 31)
    density_key, count_key, pick_key = jax.random.split(base_key, 3)
    tile_index, own_index, side_index, peer_index = view_grid()
    density = jax.random.randint(density_key, (TILES,), 1, 5)
    raw_counts = jax.random.randint(count_key, (TILES, OWNERS, 3, OWNERS), 0, CAP + 1)
    raw_counts = jnp.minimum(CAP, raw_counts * density[:, None, None, None] // 2)
    canonical, valid_view = view_masks()
    counts = jnp.where(canonical, raw_counts, mirror_view_drawn(raw_counts))
    counts = jnp.where(valid_view, counts, 0)
    chosen = jax.random.randint(pick_key, (), 0, TILES)
    full_pair = (tile_index == chosen) & (side_index == 1) & ((own_index == 0) & (peer_index == 1) | (own_index == 1) & (peer_index == 0))
    return jnp.where(full_pair, CAP, counts).astype(jnp.int32)


def draw_cross_weight(key, part):
    base_key = jax.random.fold_in(key, 37)
    raw_weight = jnp.exp(jax.random.uniform(base_key, (TILES, OWNERS, 3, OWNERS, CAP), jnp.float32, math.log(0.1), math.log(0.3)))
    canonical, valid_view = view_masks()
    return jnp.where(canonical[..., None], raw_weight, mirror_view_drawn(raw_weight)).astype(jnp.float32)


def draw_right_side(key, part):
    noise_key, offset_key = jax.random.split(jax.random.fold_in(key, 41), 2)
    noise_part = jnp.clip(jax.random.normal(noise_key, (POINTS, DATES), jnp.float32), -6.0, 6.0)
    offset = jax.random.uniform(offset_key, (1, DATES), jnp.float32, -1.5, 1.5)
    return (noise_part + offset).astype(jnp.float32)


def tile_parts(base_key):
    diag_key, tile_key = jax.random.split(base_key)
    diagonal_values = jnp.exp(jax.random.uniform(diag_key, (BLOCKS, BLK), jnp.float32, 0.0, math.log(2.0)))
    uniform_part = jax.random.uniform(tile_key, (BLOCKS, BLK, BLK), jnp.float32)
    symmetric = 0.5 * (uniform_part + jnp.swapaxes(uniform_part, 1, 2))
    identity = jnp.eye(BLK, dtype=jnp.float32)
    coupling = 0.7 / (BLK - 1) * symmetric * (1.0 - identity)
    diagonal_tile = identity * diagonal_values[:, :, None] - coupling
    smoothing = 0.6 * (identity / diagonal_values[:, :, None] + coupling / (diagonal_values[:, :, None] * diagonal_values[:, None, :]))
    return (diagonal_tile, smoothing)


def draw_diag_tiles(key, part):
    return tile_parts(jax.random.fold_in(key, 43))[0].astype(jnp.float32)


def draw_smoother(key, part):
    return tile_parts(jax.random.fold_in(key, 43))[1].astype(jnp.float32)


def draw_coarse_inverse(key, part):
    diag_key, off_key = jax.random.split(jax.random.fold_in(key, 47))
    scale_value = 1.0 / (0.7 * BLK * NB_DEV)
    diagonal_values = scale_value * jnp.exp(jax.random.uniform(diag_key, (NAGG,), jnp.float32, math.log(0.5), math.log(2.0)))
    off_part = jnp.clip(jax.random.normal(off_key, (NAGG, NAGG), jnp.float32), -6.0, 6.0) * (0.25 * scale_value / math.sqrt(NAGG))
    identity = jnp.eye(NAGG, dtype=jnp.float32)
    return (identity * diagonal_values[:, None] + off_part * (1.0 - identity)).astype(jnp.float32)


def set_ends(entries, key, least, high):
    shape = entries.shape
    place = [jax.random.randint(jax.random.fold_in(key, axis), (), 0, shape[axis]) for axis in range(len(shape))]
    entries = entries.at[tuple(place)].set(least)
    longest = shape.index(max(shape))
    place[longest] = (place[longest] + 1) % shape[longest]
    return entries.at[tuple(place)].set(high)


def block_levels(own_key, extent, pieces, low, largest):
    factor_of, own = 1.0, jax.random.fold_in(own_key, 6)
    for dim, blocks in pieces:
        draws = jnp.exp(jax.random.uniform(jax.random.fold_in(own, dim), (blocks,), jnp.float32, low / len(pieces), largest / len(pieces)))
        factor_of = factor_of * jnp.repeat(draws, extent[dim] // blocks).reshape([-1 if axis == dim else 1 for axis in range(len(extent))])
    return factor_of


def choose_distinct(rng, rows, count, top, lift):
    order = jax.random.permutation(jax.random.fold_in(rng, 1), count)
    boost = order
    for power in range(3):
        boost = boost * boost // count
    boost = boost * lift // count
    lots = jax.random.randint(jax.random.fold_in(rng, 2), (rows, count), 0, 4096) + boost
    sure = jax.random.permutation(jax.random.fold_in(rng, 3), rows)[jnp.arange(count) % rows]
    lots = jnp.where(jnp.arange(rows)[:, None] == sure[None, :], 1 << 14, lots)
    merit = lots * count + jnp.arange(count)
    return lax.top_k(merit.astype(jnp.int32), top)[1].astype(jnp.int32)


def setup_inputs(seed: int = 0) -> dict:
    arg_keys = jax.random.split(jax.random.key(seed), 12)
    right_side = draw_right_side(jax.random.fold_in(arg_keys[11], 71), 0)
    diag_tiles = draw_diag_tiles(jax.random.fold_in(arg_keys[11], 71), 0)
    smoother = draw_smoother(jax.random.fold_in(arg_keys[11], 71), 0)
    coupling_tiles = jnp.clip(-0.003125 + 0.003125 * jax.random.uniform(arg_keys[3], (COUPLES, BLK, BLK), jnp.float32) ** block_levels(arg_keys[3], (COUPLES, BLK, BLK), ((0, 32),), -0.2, 0.2), -0.003125, 0.0)
    tile_rows = set_ends(jax.random.randint(arg_keys[4], (COUPLES,), 0, NB_DEV), jax.random.fold_in(arg_keys[4], 1), 0, NB_DEV - 1).astype(jnp.int32)
    tile_cols = set_ends(jax.random.randint(arg_keys[5], (COUPLES,), 0, NB_DEV), jax.random.fold_in(arg_keys[5], 1), 0, NB_DEV - 1).astype(jnp.int32)
    cross_end = set_ends(jax.random.randint(arg_keys[6], (TILES, OWNERS, 3, OWNERS, CAP), 0, PTS_DEV), jax.random.fold_in(arg_keys[6], 1), 0, PTS_DEV - 1).astype(jnp.int32)
    cross_count = draw_cross_count(jax.random.fold_in(arg_keys[11], 71), 0)
    cross_weight = draw_cross_weight(jax.random.fold_in(arg_keys[11], 71), 0)
    block_agg = choose_distinct(arg_keys[9], BLOCKS, NAGG, 1, 256)
    coarse_inverse = draw_coarse_inverse(jax.random.fold_in(arg_keys[11], 71), 0)
    return dict(right_side=right_side, diag_tiles=diag_tiles, smoother=smoother, coupling_tiles=coupling_tiles, tile_rows=tile_rows, tile_cols=tile_cols, cross_end=cross_end, cross_count=cross_count, cross_weight=cross_weight, block_agg=block_agg, coarse_inverse=coarse_inverse)


def mirror_view(values):
    tile_index = jnp.arange(TILES, dtype=jnp.int32)[:, None, None, None]
    own_index = jnp.arange(OWNERS, dtype=jnp.int32)[None, :, None, None]
    side_index = jnp.arange(3, dtype=jnp.int32)[None, None, :, None]
    peer_index = jnp.arange(OWNERS, dtype=jnp.int32)[None, None, None, :]
    source_tile = jnp.clip(tile_index + side_index - 1, 0, TILES - 1)
    return values[source_tile, peer_index, 2 - side_index, own_index]


def reference(right_side, diag_tiles, smoother, coupling_tiles, tile_rows, tile_cols, cross_end, cross_count, cross_weight, block_agg, coarse_inverse):
    highest = lax.Precision.HIGHEST
    tile_index = jnp.arange(TILES, dtype=jnp.int32)[:, None, None, None]
    own_index = jnp.arange(OWNERS, dtype=jnp.int32)[None, :, None, None]
    side_index = jnp.arange(3, dtype=jnp.int32)[None, None, :, None]
    peer_index = jnp.arange(OWNERS, dtype=jnp.int32)[None, None, None, :]
    device_index = tile_index * OWNERS + own_index
    source_tile = jnp.clip(tile_index + side_index - 1, 0, TILES - 1)
    peer_device = source_tile * OWNERS + peer_index
    tail_index = ((device_index * PTS_DEV)[..., None] + cross_end).reshape(-1).astype(jnp.int32)
    head_index = ((peer_device * PTS_DEV)[..., None] + mirror_view(cross_end)).reshape(-1).astype(jnp.int32)
    live_mask = jnp.arange(CAP, dtype=jnp.int32) < cross_count[..., None]
    arc_weight = jnp.where(live_mask, cross_weight, jnp.zeros_like(cross_weight)).reshape(-1)
    owner_base = ((jnp.arange(COUPLES, dtype=jnp.int32) // NT_DEV) * NB_DEV).astype(jnp.int32)
    row_blocks = (owner_base + tile_rows).astype(jnp.int32)
    col_blocks = (owner_base + tile_cols).astype(jnp.int32)

    def operate(field_rows):
        field_blocks = field_rows.reshape(BLOCKS, BLK, DATES)
        local_part = jnp.einsum("bij,bjd->bid", diag_tiles, field_blocks, precision=highest)
        coupled = jnp.einsum("cij,cjd->cid", coupling_tiles, field_blocks[col_blocks], precision=highest)
        local_part = local_part + jax.ops.segment_sum(coupled, row_blocks, num_segments=BLOCKS)
        arc_terms = arc_weight[:, None] * (field_rows[tail_index] - field_rows[head_index])
        return local_part.reshape(POINTS, DATES) + jax.ops.segment_sum(arc_terms, tail_index, num_segments=POINTS)

    def smooth(field_rows, residual):
        update = jnp.einsum("bij,bjd->bid", smoother, residual.reshape(BLOCKS, BLK, DATES), precision=highest)
        return field_rows + update.reshape(POINTS, DATES)

    iterate = smooth(jnp.zeros_like(right_side), right_side)
    for repeat in range(SWEEPS - 1):
        iterate = smooth(iterate, right_side - operate(iterate))
    residual = right_side - operate(iterate)
    block_sums = residual.reshape(BLOCKS, BLK, DATES).sum(axis=1)
    aggregate = block_agg[:, 0].astype(jnp.int32)
    coarse_res = jax.ops.segment_sum(block_sums, aggregate, num_segments=NAGG)
    correction = jnp.dot(coarse_inverse, coarse_res, precision=highest)
    iterate = (iterate.reshape(BLOCKS, BLK, DATES) + correction[aggregate][:, None, :]).reshape(POINTS, DATES)
    for repeat in range(SWEEPS):
        iterate = smooth(iterate, right_side - operate(iterate))
    return iterate
```

```python
import functools

import jax
import jax.numpy as jnp
from jax import lax
from jax.experimental import pallas as pl
from jax.experimental.pallas import tpu as pltpu
from jax.sharding import PartitionSpec as P

MESH = pl.DeviceIdType.MESH
F32 = jnp.float32
BF16 = jnp.bfloat16
HIGHEST = lax.Precision.HIGHEST


def split(x):
    hi = x.astype(BF16)
    lo = (x - hi.astype(F32)).astype(BF16)
    return hi, lo


def kernel(
    tiles, owners, nb, nt, blk, dates, cap, nagg,
    ends_s, weight_s, cols_s, prev_s, last_s,
    right_h, diag_h, smooth_h, coup_h,
    ends_v, weight_v, agg_col, agg_row, cinv,
    out_ref,
    right, stage_d, stage_s, stage_c,
    v, vcat, wsm, wop, part, hot, terms, send, recv,
    bsum, partial_ref, red_in, red_sum, all_in, full, ci, corr_rows,
    in_sem, send_sem, recv_sem,
    ra_send, ra_recv, rt_send, rt_recv, rg_send, rg_recv,
    ca_send, ca_recv, ct_send, ct_recv,
):
    t = lax.axis_index("tile")
    g = lax.axis_index("agg")
    slots = 3 * owners * cap
    rows = nagg // owners

    loads = [
        pltpu.make_async_copy(right_h, right, in_sem.at[0]),
        pltpu.make_async_copy(smooth_h, stage_s, in_sem.at[1]),
        pltpu.make_async_copy(diag_h, stage_d, in_sem.at[2]),
        pltpu.make_async_copy(coup_h, stage_c, in_sem.at[3]),
    ]
    for load in loads:
        load.start()

    def section(i):
        k = i // owners
        h = lax.rem(g + lax.rem(i, owners), owners)
        other = t + k - 1
        valid = (other >= 0) & (other < tiles) & jnp.logical_not((k == 1) & (h == g))
        return k, h, other, valid

    barrier = pltpu.get_barrier_semaphore()

    @pl.loop(0, 3 * owners)
    def _(i):
        k, h, other, valid = section(i)

        @pl.when(valid)
        def _():
            pl.semaphore_signal(barrier, inc=1, device_id=(other, h), device_id_type=MESH)

    @pl.loop(1, tiles)
    def _(d):
        pl.semaphore_signal(
            barrier, inc=1, device_id=(lax.rem(t + d, tiles), g), device_id_type=MESH
        )

    @pl.loop(0, 3 * owners)
    def _(i):
        k, h, other, valid = section(i)

        @pl.when(jnp.logical_not(valid))
        def _():
            for turn in range(recv.shape[0]):
                recv[turn, k * owners + h] = jnp.zeros((cap, dates), F32)

    ci[t * owners + g] = jnp.zeros((1, ci.shape[2]), F32)
    ci[t * owners + g, :, 0:nagg] = cinv[...]

    ends = ends_v[...]
    weight = weight_v[...]
    eye = (
        lax.broadcasted_iota(jnp.int32, (blk, blk), 0)
        == lax.broadcasted_iota(jnp.int32, (blk, blk), 1)
    )

    def make_hot(b):
        pick = (lax.broadcasted_iota(jnp.int32, (blk, slots), 0) + b * blk) == ends
        one = jnp.where(pick, 1.0, 0.0).astype(BF16)
        hot[b, :, 0:slots] = one
        hot[b, :, slots : 2 * slots] = one
        return jnp.sum(jnp.where(pick, weight, 0.0), axis=1, keepdims=True)

    def put3(ref, b, x):
        hi, lo = split(x)
        ref[b, 0:blk, :] = hi
        ref[b, blk : 2 * blk, :] = hi
        ref[b, 2 * blk : 3 * blk, :] = lo

    def put3w(ref, b, x):
        hi, lo = split(x)
        ref[b, :, 0:blk] = hi
        ref[b, :, blk : 2 * blk] = lo
        ref[b, :, 2 * blk : 3 * blk] = hi

    def product(w, x):
        return jnp.dot(w, x, preferred_element_type=F32)

    def cat3(x):
        hi, lo = split(x)
        return jnp.concatenate([hi, hi, lo], axis=0)

    loads[0].wait()
    loads[1].wait()

    @pl.loop(0, nb, unroll=2)
    def _(b):
        put3w(wsm, b, stage_s[b])
        new = product(wsm[b], cat3(right[b]))
        v[pl.ds(pl.multiple_of(b * blk, blk), blk), :] = new
        put3(vcat, b, new)

    nvalid = (
        (owners - 1)
        + owners * (t > 0).astype(jnp.int32)
        + owners * (t < tiles - 1).astype(jnp.int32)
    )
    pl.semaphore_wait(barrier, nvalid + tiles - 1)

    def ci_copy_agg(d):
        h = lax.rem(g + d, owners)
        return pltpu.make_async_remote_copy(
            src_ref=ci.at[t * owners + g],
            dst_ref=ci.at[t * owners + g],
            send_sem=ca_send.at[d],
            recv_sem=ca_recv.at[d],
            device_id=(t, h),
            device_id_type=MESH,
        )

    def ci_copy_tile(d):
        return pltpu.make_async_remote_copy(
            src_ref=ci.at[pl.ds(t * owners, owners)],
            dst_ref=ci.at[pl.ds(t * owners, owners)],
            send_sem=ct_send.at[d],
            recv_sem=ct_recv.at[d],
            device_id=(lax.rem(t + d, tiles), g),
            device_id_type=MESH,
        )

    for d in range(1, owners):
        ci_copy_agg(d).start()

    def halo_copy(turn, i):
        k, h, other, valid = section(i)
        return valid, pltpu.make_async_remote_copy(
            src_ref=send.at[turn, i],
            dst_ref=recv.at[turn, (2 - k) * owners + g],
            send_sem=send_sem.at[turn, i],
            recv_sem=recv_sem.at[turn, (2 - k) * owners + g],
            device_id=(other, h),
            device_id_type=MESH,
        )

    def halo_start(turn):
        @pl.loop(0, 3 * owners)
        def _(i):
            k, h, other, valid = section(i)
            base = (k * owners + h) * cap
            for s in range(cap):
                row = v[pl.ds(ends_s[base + s], 1), :]
                send[turn, i, s : s + 1, :] = row * weight_s[base + s]
            _, copy = halo_copy(turn, i)

            @pl.when(valid)
            def _():
                copy.start()

    def halo_finish(turn):
        @pl.loop(0, 3 * owners)
        def _(i):
            k, h, other, valid = section(i)

            @pl.when(valid)
            def _():
                src = k * owners + h
                pltpu.make_async_remote_copy(
                    src_ref=send.at[turn, i],
                    dst_ref=recv.at[turn, src],
                    send_sem=send_sem.at[turn, i],
                    recv_sem=recv_sem.at[turn, src],
                    device_id=(other, h),
                    device_id_type=MESH,
                ).wait()

        @pl.loop(0, 3 * owners)
        def _(i):
            hi, lo = split(recv[turn, i])
            at = pl.multiple_of(i * cap, cap)
            terms[pl.ds(at, cap), :] = hi
            terms[pl.ds(slots + at, cap), :] = lo

    def local_part():
        @pl.loop(0, nb, unroll=4)
        def _(b):
            part[b] = product(wop[b], vcat[b])

        @pl.loop(0, nt, unroll=4)
        def _(c):
            part[nb + c] = part[prev_s[c]] + product(wop[nb + c], vcat[cols_s[c]])

    def residual(b):
        return right[b] - part[last_s[b]] + product(hot[b], terms[...])

    def sweep(final):
        @pl.loop(0, nb, unroll=4)
        def _(b):
            at = pl.ds(pl.multiple_of(b * blk, blk), blk)
            new = v[at, :] + product(wsm[b], cat3(residual(b)))
            if final:
                out_ref[at, :] = new
            else:
                v[at, :] = new
                put3(vcat, b, new)

    halo_start(0)
    loads[2].wait()
    loads[3].wait()

    @pl.loop(0, nb)
    def _(b):
        tail = make_hot(b)
        put3w(wop, b, stage_d[b] + jnp.where(eye, tail, 0.0))

    @pl.loop(0, nt, unroll=2)
    def _(c):
        put3w(wop, nb + c, stage_c[c])

    local_part()
    for d in range(1, owners):
        ci_copy_agg(d).wait()

    @pl.loop(1, tiles)
    def _(d):
        ci_copy_tile(d).start()

    halo_finish(0)
    sweep(False)

    halo_start(1)
    local_part()
    halo_finish(1)

    @pl.loop(0, nb, unroll=4)
    def _(b):
        bsum[pl.ds(b, 1), :] = jnp.sum(residual(b), axis=0, keepdims=True)

    pick_t = jnp.where(
        lax.broadcasted_iota(jnp.int32, (nagg, nb), 0) == agg_row[...], 1.0, 0.0
    )
    partial_ref[...] = jnp.dot(
        pick_t, bsum[...], preferred_element_type=F32, precision=HIGHEST
    )

    def red_copy(d):
        h = lax.rem(g + d, owners)
        return pltpu.make_async_remote_copy(
            src_ref=partial_ref.at[pl.ds(pl.multiple_of(h * rows, rows), rows)],
            dst_ref=red_in.at[d],
            send_sem=ra_send.at[d],
            recv_sem=ra_recv.at[d],
            device_id=(t, h),
            device_id_type=MESH,
        )

    for d in range(1, owners):
        red_copy(d).start()
    total = partial_ref[pl.ds(pl.multiple_of(g * rows, rows), rows), :]
    for d in range(1, owners):
        red_copy(d).wait()
        total = total + red_in[d]
    red_sum[...] = total

    def tile_copy(d):
        return pltpu.make_async_remote_copy(
            src_ref=red_sum,
            dst_ref=all_in.at[d],
            send_sem=rt_send.at[d],
            recv_sem=rt_recv.at[d],
            device_id=(lax.rem(t + d, tiles), g),
            device_id_type=MESH,
        )

    @pl.loop(1, tiles)
    def _(d):
        tile_copy(d).start()

    all_in[0] = red_sum[...]

    @pl.loop(1, tiles)
    def _(d):
        tile_copy(d).wait()

    own_rows = pl.ds(pl.multiple_of(g * rows, rows), rows)
    full[own_rows, :] = jnp.sum(all_in[...], axis=0)

    def gather_copy(d):
        h = lax.rem(g + d, owners)
        return pltpu.make_async_remote_copy(
            src_ref=full.at[own_rows],
            dst_ref=full.at[own_rows],
            send_sem=rg_send.at[d],
            recv_sem=rg_recv.at[d],
            device_id=(t, h),
            device_id_type=MESH,
        )

    for d in range(1, owners):
        gather_copy(d).start()

    @pl.loop(1, tiles)
    def _(d):
        ci_copy_tile(d).wait()

    for d in range(1, owners):
        gather_copy(d).wait()

    inverse = ci[...].reshape(nagg, ci.shape[2])[:, 0:nagg]
    corr = jnp.dot(inverse, full[...], preferred_element_type=F32, precision=HIGHEST)
    pick = jnp.where(
        lax.broadcasted_iota(jnp.int32, (nb, nagg), 1) == agg_col[...], 1.0, 0.0
    )
    corr_rows[...] = jnp.dot(pick, corr, preferred_element_type=F32, precision=HIGHEST)

    @pl.loop(0, nb, unroll=2)
    def _(b):
        at = pl.ds(pl.multiple_of(b * blk, blk), blk)
        new = v[at, :] + corr_rows[pl.ds(b, 1), :]
        v[at, :] = new
        put3(vcat, b, new)

    halo_start(2)
    local_part()
    halo_finish(2)
    sweep(False)
    halo_start(3)
    local_part()
    halo_finish(3)
    sweep(True)


def local(
    tiles, right_side, diag_tiles, smoother, coupling_tiles, tile_rows, tile_cols,
    cross_end, cross_count, cross_weight, block_agg, coarse_inverse,
):
    nb, blk, _ = diag_tiles.shape
    nt = coupling_tiles.shape[0]
    points, dates = right_side.shape
    owners, cap = cross_end.shape[3:]
    nagg = coarse_inverse.shape[1]
    slots = 3 * owners * cap
    rows = nagg // owners
    turns = 4

    ends = cross_end.reshape(slots)
    live = jnp.arange(cap, dtype=jnp.int32) < cross_count[0, 0][:, :, None]
    weight = jnp.where(live, cross_weight[0, 0], 0.0).reshape(slots)
    order = jnp.arange(nt, dtype=jnp.int32)
    same = (tile_rows[:, None] == tile_rows[None, :]) & (order[None, :] < order[:, None])
    prev = jnp.maximum(
        jnp.max(jnp.where(same, order[None, :] + nb, 0), axis=1), tile_rows
    )
    block = jnp.arange(nb, dtype=jnp.int32)
    last = jnp.maximum(
        jnp.max(jnp.where(tile_rows[None, :] == block[:, None], order[None, :] + nb, 0), axis=1),
        block,
    )
    smem = pl.BlockSpec(memory_space=pltpu.SMEM)
    vmem = pl.BlockSpec(memory_space=pltpu.VMEM)
    hbm = pl.BlockSpec(memory_space=pl.ANY)
    dma = pltpu.SemaphoreType.DMA
    return pl.pallas_call(
        functools.partial(kernel, tiles, owners, nb, nt, blk, dates, cap, nagg),
        out_shape=jax.ShapeDtypeStruct((points, dates), F32),
        in_specs=[smem] * 5 + [hbm] * 4 + [vmem] * 5,
        out_specs=vmem,
        scratch_shapes=[
            pltpu.VMEM((nb, blk, dates), F32),
            pltpu.VMEM((nb, blk, blk), F32),
            pltpu.VMEM((nb, blk, blk), F32),
            pltpu.VMEM((nt, blk, blk), F32),
            pltpu.VMEM((points, dates), F32),
            pltpu.VMEM((nb, 3 * blk, dates), BF16),
            pltpu.VMEM((nb, blk, 3 * blk), BF16),
            pltpu.VMEM((nb + nt, blk, 3 * blk), BF16),
            pltpu.VMEM((nb + nt, blk, dates), F32),
            pltpu.VMEM((nb, blk, 2 * slots), BF16),
            pltpu.VMEM((2 * slots, dates), BF16),
            pltpu.VMEM((turns, 3 * owners, cap, dates), F32),
            pltpu.VMEM((turns, 3 * owners, cap, dates), F32),
            pltpu.VMEM((nb, dates), F32),
            pltpu.VMEM((nagg, dates), F32),
            pltpu.VMEM((owners, rows, dates), F32),
            pltpu.VMEM((rows, dates), F32),
            pltpu.VMEM((tiles, rows, dates), F32),
            pltpu.VMEM((nagg, dates), F32),
            pltpu.VMEM((nagg, 1, 128 * ((nagg + 127) // 128)), F32),
            pltpu.VMEM((nb, dates), F32),
            dma((4,)),
            dma((turns, 3 * owners)),
            dma((turns, 3 * owners)),
            dma((owners,)), dma((owners,)),
            dma((tiles,)), dma((tiles,)),
            dma((owners,)), dma((owners,)),
            dma((owners,)), dma((owners,)),
            dma((tiles,)), dma((tiles,)),
        ],
        compiler_params=pltpu.CompilerParams(
            collective_id=0, has_side_effects=True, vmem_limit_bytes=56 * 1024 * 1024
        ),
        cost_estimate=pl.CostEstimate(
            flops=8 * 256 * blk * blk * dates, bytes_accessed=8 << 20, transcendentals=0
        ),
    )(
        ends, weight, tile_cols, prev, last,
        right_side.reshape(nb, blk, dates), diag_tiles, smoother, coupling_tiles,
        ends.reshape(1, slots), weight.reshape(1, slots),
        block_agg, block_agg.reshape(1, nb), coarse_inverse,
    )


def solution(mesh):
    both = ("tile", "agg")
    placed = (
        P(both, None),
        P(both, None, None),
        P(both, None, None),
        P(both, None, None),
        P(both),
        P(both),
        P("tile", "agg", None, None, None),
        P("tile", "agg", None, None),
        P("tile", "agg", None, None, None),
        P(both, None),
        P(both, None),
    )
    return jax.shard_map(
        functools.partial(local, mesh.shape["tile"]),
        mesh=mesh, in_specs=placed, out_specs=P(both, None), check_vma=False,
    )
```

```python
import functools

import jax
import jax.numpy as jnp
from jax import lax
from jax.experimental import pallas as pl
from jax.experimental.pallas import tpu as pltpu
from jax.sharding import PartitionSpec as P

MESH = pl.DeviceIdType.MESH
F32 = jnp.float32
BF16 = jnp.bfloat16
HIGHEST = lax.Precision.HIGHEST


def split(x):
    hi = x.astype(BF16)
    lo = (x - hi.astype(F32)).astype(BF16)
    return hi, lo


def kernel(
    tiles, owners, nb, nt, blk, dates, cap, nagg,
    ends_s, count_s, raw_s, rows_s, cols_s, agg_s,
    right_h, diag_h, smooth_h, coup_h,
    ends_v, raw_v, agg_row, cinv,
    out_ref,
    right, stage_d, stage_s, stage_c,
    v, vcat, wsm, wop, part, hot, terms, send, recv,
    bsum, partial_ref, red_in, red_sum, all_in, full, ci, corr_ref,
    ends_row, weight_row, prev_s, last_s, resid, flat, ap3, corr3, send_p, recv_p,
    in_sem, send_sem, recv_sem, psend_sem, precv_sem,
    ra_send, ra_recv, rt_send, rt_recv, rg_send, rg_recv,
    ca_send, ca_recv, ct_send, ct_recv,
):
    t = lax.axis_index("tile")
    g = lax.axis_index("agg")
    slots = 3 * owners * cap
    rows = nagg // owners
    lanes = recv_p.shape[2]

    loads = [
        pltpu.make_async_copy(right_h, right, in_sem.at[0]),
        pltpu.make_async_copy(smooth_h, stage_s, in_sem.at[1]),
        pltpu.make_async_copy(diag_h, stage_d, in_sem.at[2]),
        pltpu.make_async_copy(coup_h, stage_c, in_sem.at[3]),
    ]
    for load in loads:
        load.start()

    def section(i):
        k = i // owners
        h = lax.rem(g + lax.rem(i, owners), owners)
        other = t + k - 1
        valid = (other >= 0) & (other < tiles) & jnp.logical_not((k == 1) & (h == g))
        return k, h, other, valid

    barrier = pltpu.get_barrier_semaphore()

    @pl.loop(0, 3 * owners)
    def _(i):
        k, h, other, valid = section(i)

        @pl.when(valid)
        def _():
            pl.semaphore_signal(barrier, inc=1, device_id=(other, h), device_id_type=MESH)

    @pl.loop(1, tiles)
    def _(d):
        pl.semaphore_signal(
            barrier, inc=1, device_id=(lax.rem(t + d, tiles), g), device_id_type=MESH
        )

    @pl.loop(0, 3 * owners)
    def _(i):
        k, h, other, valid = section(i)

        @pl.when(jnp.logical_not(valid))
        def _():
            for turn in range(recv.shape[0]):
                recv[turn, k * owners + h] = jnp.zeros((cap, dates), F32)
            recv_p[k * owners + h] = jnp.zeros((cap, lanes), F32)

    ci[t * owners + g] = jnp.zeros((1, ci.shape[2]), F32)
    ci[t * owners + g, :, 0:nagg] = cinv[...]

    for k in range(3):
        for h in range(owners):
            at = (k * owners + h) * cap
            ends_row[:, at : at + cap] = ends_v[0, 0, k, h : h + 1, :]
            alive = lax.broadcasted_iota(jnp.int32, (1, cap), 1) < count_s[0, 0, k, h]
            weight_row[:, at : at + cap] = jnp.where(alive, raw_v[0, 0, k, h : h + 1, :], 0.0)

    @pl.loop(0, nt)
    def _(c):
        row = rows_s[c]
        found = row
        for e in range(nt):
            found = jnp.where((rows_s[e] == row) & (e < c), nb + e, found)
        prev_s[c] = found

    @pl.loop(0, nb)
    def _(b):
        found = b
        for e in range(nt):
            found = jnp.where(rows_s[e] == b, nb + e, found)
        last_s[b] = found

    ends = ends_row[...]
    weight = weight_row[...]
    eye = (
        lax.broadcasted_iota(jnp.int32, (blk, blk), 0)
        == lax.broadcasted_iota(jnp.int32, (blk, blk), 1)
    )

    def make_hot(b):
        pick = (lax.broadcasted_iota(jnp.int32, (blk, slots), 0) + b * blk) == ends
        one = jnp.where(pick, 1.0, 0.0).astype(BF16)
        hot[b, :, 0:slots] = one
        hot[b, :, slots : 2 * slots] = one
        return jnp.sum(jnp.where(pick, weight, 0.0), axis=1, keepdims=True)

    def put3(ref, b, x):
        hi, lo = split(x)
        ref[b, 0:blk, :] = hi
        ref[b, blk : 2 * blk, :] = hi
        ref[b, 2 * blk : 3 * blk, :] = lo

    def put3w(ref, b, x):
        hi, lo = split(x)
        ref[b, :, 0:blk] = hi
        ref[b, :, blk : 2 * blk] = lo
        ref[b, :, 2 * blk : 3 * blk] = hi

    def product(w, x):
        return jnp.dot(w, x, preferred_element_type=F32)

    def cat3(x):
        hi, lo = split(x)
        return jnp.concatenate([hi, hi, lo], axis=0)

    loads[0].wait()
    loads[1].wait()

    @pl.loop(0, nb, unroll=2)
    def _(b):
        put3w(wsm, b, stage_s[b])
        new = product(wsm[b], cat3(right[b]))
        v[pl.ds(pl.multiple_of(b * blk, blk), blk), :] = new
        put3(vcat, b, new)

    nvalid = (
        (owners - 1)
        + owners * (t > 0).astype(jnp.int32)
        + owners * (t < tiles - 1).astype(jnp.int32)
    )
    pl.semaphore_wait(barrier, nvalid + tiles - 1)

    def ci_copy_agg(d):
        h = lax.rem(g + d, owners)
        return pltpu.make_async_remote_copy(
            src_ref=ci.at[t * owners + g],
            dst_ref=ci.at[t * owners + g],
            send_sem=ca_send.at[d],
            recv_sem=ca_recv.at[d],
            device_id=(t, h),
            device_id_type=MESH,
        )

    def ci_copy_tile(d):
        return pltpu.make_async_remote_copy(
            src_ref=ci.at[pl.ds(t * owners, owners)],
            dst_ref=ci.at[pl.ds(t * owners, owners)],
            send_sem=ct_send.at[d],
            recv_sem=ct_recv.at[d],
            device_id=(lax.rem(t + d, tiles), g),
            device_id_type=MESH,
        )

    for d in range(1, owners):
        ci_copy_agg(d).start()

    def halo_copy(turn, i):
        k, h, other, valid = section(i)
        return valid, pltpu.make_async_remote_copy(
            src_ref=send.at[turn, i],
            dst_ref=recv.at[turn, (2 - k) * owners + g],
            send_sem=send_sem.at[turn, i],
            recv_sem=recv_sem.at[turn, (2 - k) * owners + g],
            device_id=(other, h),
            device_id_type=MESH,
        )

    def halo_start(turn):
        @pl.loop(0, 3 * owners)
        def _(i):
            k, h, other, valid = section(i)
            count = count_s[0, 0, k, h]
            for s in range(cap):
                end = ends_s[0, 0, k, h, s]
                scale = jnp.where(s < count, raw_s[0, 0, k, h, s], 0.0)
                send[turn, i, s : s + 1, :] = v[pl.ds(end, 1), :] * scale
            _, copy = halo_copy(turn, i)

            @pl.when(valid)
            def _():
                copy.start()

    def basis_copy(i):
        k, h, other, valid = section(i)
        return pltpu.make_async_remote_copy(
            src_ref=send_p.at[i],
            dst_ref=recv_p.at[(2 - k) * owners + g],
            send_sem=psend_sem.at[i],
            recv_sem=precv_sem.at[(2 - k) * owners + g],
            device_id=(other, h),
            device_id_type=MESH,
        )

    def basis_start():
        lane = lax.broadcasted_iota(jnp.int32, (1, lanes), 1)

        @pl.loop(0, 3 * owners)
        def _(i):
            k, h, other, valid = section(i)
            count = count_s[0, 0, k, h]
            for s in range(cap):
                target = agg_s[0, lax.div(ends_s[0, 0, k, h, s], blk)]
                scale = jnp.where(s < count, raw_s[0, 0, k, h, s], 0.0)
                send_p[i, s : s + 1, :] = jnp.where(lane == target, scale, 0.0)

            @pl.when(valid)
            def _():
                basis_copy(i).start()

    def basis_finish():
        @pl.loop(0, 3 * owners)
        def _(i):
            k, h, other, valid = section(i)

            @pl.when(valid)
            def _():
                src = k * owners + h
                pltpu.make_async_remote_copy(
                    src_ref=send_p.at[i],
                    dst_ref=recv_p.at[src],
                    send_sem=psend_sem.at[i],
                    recv_sem=precv_sem.at[src],
                    device_id=(other, h),
                    device_id_type=MESH,
                ).wait()

        lane = lax.broadcasted_iota(jnp.int32, (1, lanes), 1)

        @pl.loop(0, nb, unroll=2)
        def _(b):
            total = jnp.sum(stage_d[b], axis=1, keepdims=True)
            flat[b] = jnp.where(lane == agg_s[0, b], total, 0.0)

        @pl.loop(0, nt, unroll=2)
        def _(c):
            total = jnp.sum(stage_c[c], axis=1, keepdims=True)
            flat[nb + c] = flat[prev_s[c]] + jnp.where(
                lane == agg_s[0, cols_s[c]], total, 0.0
            )

        hi, lo = split(recv_p[...].reshape(slots, lanes))
        heads = jnp.concatenate([hi, lo], axis=0)

        @pl.loop(0, nb, unroll=2)
        def _(b):
            hi, lo = split(flat[last_s[b]] - product(hot[b], heads))
            ap3[b, :, 0:lanes] = hi
            ap3[b, :, lanes : 2 * lanes] = lo
            ap3[b, :, 2 * lanes : 3 * lanes] = hi

    def halo_finish(turn):
        @pl.loop(0, 3 * owners)
        def _(i):
            k, h, other, valid = section(i)

            @pl.when(valid)
            def _():
                src = k * owners + h
                pltpu.make_async_remote_copy(
                    src_ref=send.at[turn, i],
                    dst_ref=recv.at[turn, src],
                    send_sem=send_sem.at[turn, i],
                    recv_sem=recv_sem.at[turn, src],
                    device_id=(other, h),
                    device_id_type=MESH,
                ).wait()

        @pl.loop(0, 3 * owners)
        def _(i):
            hi, lo = split(recv[turn, i])
            at = pl.multiple_of(i * cap, cap)
            terms[pl.ds(at, cap), :] = hi
            terms[pl.ds(slots + at, cap), :] = lo

    def local_part():
        @pl.loop(0, nb, unroll=4)
        def _(b):
            part[b] = product(wop[b], vcat[b])

        @pl.loop(0, nt, unroll=4)
        def _(c):
            part[nb + c] = part[prev_s[c]] + product(wop[nb + c], vcat[cols_s[c]])

    def residual(b):
        return right[b] - part[last_s[b]] + product(hot[b], terms[...])

    def sweep(final):
        @pl.loop(0, nb, unroll=4)
        def _(b):
            at = pl.ds(pl.multiple_of(b * blk, blk), blk)
            new = v[at, :] + product(wsm[b], cat3(residual(b)))
            if final:
                out_ref[at, :] = new
            else:
                v[at, :] = new
                put3(vcat, b, new)

    halo_start(0)
    loads[2].wait()
    loads[3].wait()

    @pl.loop(0, nb)
    def _(b):
        tail = make_hot(b)
        tile = stage_d[b] + jnp.where(eye, tail, 0.0)
        stage_d[b] = tile
        put3w(wop, b, tile)

    @pl.loop(0, nt, unroll=2)
    def _(c):
        put3w(wop, nb + c, stage_c[c])

    local_part()
    for d in range(1, owners):
        ci_copy_agg(d).wait()

    @pl.loop(1, tiles)
    def _(d):
        ci_copy_tile(d).start()

    halo_finish(0)
    sweep(False)

    halo_start(1)
    basis_start()
    local_part()
    halo_finish(1)

    @pl.loop(0, nb, unroll=4)
    def _(b):
        rest = residual(b)
        resid[b] = rest
        bsum[pl.ds(b, 1), :] = jnp.sum(rest, axis=0, keepdims=True)

    pick_t = jnp.where(
        lax.broadcasted_iota(jnp.int32, (nagg, nb), 0) == agg_row[...], 1.0, 0.0
    )
    partial_ref[...] = jnp.dot(
        pick_t, bsum[...], preferred_element_type=F32, precision=HIGHEST
    )

    def red_copy(d):
        h = lax.rem(g + d, owners)
        return pltpu.make_async_remote_copy(
            src_ref=partial_ref.at[pl.ds(pl.multiple_of(h * rows, rows), rows)],
            dst_ref=red_in.at[d],
            send_sem=ra_send.at[d],
            recv_sem=ra_recv.at[d],
            device_id=(t, h),
            device_id_type=MESH,
        )

    for d in range(1, owners):
        red_copy(d).start()
    basis_finish()
    total = partial_ref[pl.ds(pl.multiple_of(g * rows, rows), rows), :]
    for d in range(1, owners):
        red_copy(d).wait()
        total = total + red_in[d]
    red_sum[...] = total

    def tile_copy(d):
        return pltpu.make_async_remote_copy(
            src_ref=red_sum,
            dst_ref=all_in.at[d],
            send_sem=rt_send.at[d],
            recv_sem=rt_recv.at[d],
            device_id=(lax.rem(t + d, tiles), g),
            device_id_type=MESH,
        )

    @pl.loop(1, tiles)
    def _(d):
        tile_copy(d).start()

    all_in[0] = red_sum[...]

    @pl.loop(1, tiles)
    def _(d):
        tile_copy(d).wait()

    own_rows = pl.ds(pl.multiple_of(g * rows, rows), rows)
    full[own_rows, :] = jnp.sum(all_in[...], axis=0)

    def gather_copy(d):
        h = lax.rem(g + d, owners)
        return pltpu.make_async_remote_copy(
            src_ref=full.at[own_rows],
            dst_ref=full.at[own_rows],
            send_sem=rg_send.at[d],
            recv_sem=rg_recv.at[d],
            device_id=(t, h),
            device_id_type=MESH,
        )

    for d in range(1, owners):
        gather_copy(d).start()

    @pl.loop(1, tiles)
    def _(d):
        ci_copy_tile(d).wait()

    for d in range(1, owners):
        gather_copy(d).wait()

    inverse = ci[...].reshape(nagg, ci.shape[2])[:, 0:nagg]
    corr = jnp.dot(inverse, full[...], preferred_element_type=F32, precision=HIGHEST)
    corr_ref[...] = jnp.zeros_like(corr_ref)
    corr_ref[0:nagg, :] = corr
    corr3[...] = cat3(corr_ref[...])

    @pl.loop(0, nb, unroll=4)
    def _(b):
        at = pl.ds(pl.multiple_of(b * blk, blk), blk)
        rest = resid[b] - product(ap3[b], corr3[...])
        new = v[at, :] + corr_ref[pl.ds(agg_s[0, b], 1), :] + product(wsm[b], cat3(rest))
        v[at, :] = new
        put3(vcat, b, new)

    halo_start(2)
    local_part()
    halo_finish(2)
    sweep(True)


def local(
    tiles, right_side, diag_tiles, smoother, coupling_tiles, tile_rows, tile_cols,
    cross_end, cross_count, cross_weight, block_agg, coarse_inverse,
):
    nb, blk, _ = diag_tiles.shape
    nt = coupling_tiles.shape[0]
    points, dates = right_side.shape
    owners, cap = cross_end.shape[3:]
    nagg = coarse_inverse.shape[1]
    slots = 3 * owners * cap
    rows = nagg // owners
    turns = 3
    lanes = 128 * ((nagg + 127) // 128)

    smem = pl.BlockSpec(memory_space=pltpu.SMEM)
    vmem = pl.BlockSpec(memory_space=pltpu.VMEM)
    hbm = pl.BlockSpec(memory_space=pl.ANY)
    dma = pltpu.SemaphoreType.DMA
    return pl.pallas_call(
        functools.partial(kernel, tiles, owners, nb, nt, blk, dates, cap, nagg),
        out_shape=jax.ShapeDtypeStruct((points, dates), F32),
        in_specs=[smem] * 6 + [hbm] * 4 + [vmem] * 4,
        out_specs=vmem,
        scratch_shapes=[
            pltpu.VMEM((nb, blk, dates), F32),
            pltpu.VMEM((nb, blk, blk), F32),
            pltpu.VMEM((nb, blk, blk), F32),
            pltpu.VMEM((nt, blk, blk), F32),
            pltpu.VMEM((points, dates), F32),
            pltpu.VMEM((nb, 3 * blk, dates), BF16),
            pltpu.VMEM((nb, blk, 3 * blk), BF16),
            pltpu.VMEM((nb + nt, blk, 3 * blk), BF16),
            pltpu.VMEM((nb + nt, blk, dates), F32),
            pltpu.VMEM((nb, blk, 2 * slots), BF16),
            pltpu.VMEM((2 * slots, dates), BF16),
            pltpu.VMEM((turns, 3 * owners, cap, dates), F32),
            pltpu.VMEM((turns, 3 * owners, cap, dates), F32),
            pltpu.VMEM((nb, dates), F32),
            pltpu.VMEM((nagg, dates), F32),
            pltpu.VMEM((owners, rows, dates), F32),
            pltpu.VMEM((rows, dates), F32),
            pltpu.VMEM((tiles, rows, dates), F32),
            pltpu.VMEM((nagg, dates), F32),
            pltpu.VMEM((nagg, 1, lanes), F32),
            pltpu.VMEM((lanes, dates), F32),
            pltpu.VMEM((1, slots), jnp.int32),
            pltpu.VMEM((1, slots), F32),
            pltpu.SMEM((nt,), jnp.int32),
            pltpu.SMEM((nb,), jnp.int32),
            pltpu.VMEM((nb, blk, dates), F32),
            pltpu.VMEM((nb + nt, blk, lanes), F32),
            pltpu.VMEM((nb, blk, 3 * lanes), BF16),
            pltpu.VMEM((3 * lanes, dates), BF16),
            pltpu.VMEM((3 * owners, cap, lanes), F32),
            pltpu.VMEM((3 * owners, cap, lanes), F32),
            dma((4,)),
            dma((turns, 3 * owners)),
            dma((turns, 3 * owners)),
            dma((3 * owners,)),
            dma((3 * owners,)),
            dma((owners,)), dma((owners,)),
            dma((tiles,)), dma((tiles,)),
            dma((owners,)), dma((owners,)),
            dma((owners,)), dma((owners,)),
            dma((tiles,)), dma((tiles,)),
        ],
        compiler_params=pltpu.CompilerParams(
            collective_id=0, has_side_effects=True, vmem_limit_bytes=56 * 1024 * 1024
        ),
        cost_estimate=pl.CostEstimate(
            flops=8 * 256 * blk * blk * dates, bytes_accessed=8 << 20, transcendentals=0
        ),
    )(
        cross_end, cross_count, cross_weight, tile_rows, tile_cols, block_agg.reshape(1, nb),
        right_side.reshape(nb, blk, dates), diag_tiles, smoother, coupling_tiles,
        cross_end, cross_weight, block_agg.reshape(1, nb), coarse_inverse,
    )


def solution(mesh):
    both = ("tile", "agg")
    placed = (
        P(both, None),
        P(both, None, None),
        P(both, None, None),
        P(both, None, None),
        P(both),
        P(both),
        P("tile", "agg", None, None, None),
        P("tile", "agg", None, None),
        P("tile", "agg", None, None, None),
        P(both, None),
        P(both, None),
    )
    return jax.shard_map(
        functools.partial(local, mesh.shape["tile"]),
        mesh=mesh, in_specs=placed, out_specs=P(both, None), check_vma=False,
    )
```

```python
import functools

import jax
import jax.numpy as jnp
from jax import lax
from jax.experimental import pallas as pl
from jax.experimental.pallas import tpu as pltpu
from jax.sharding import PartitionSpec as P

MESH = pl.DeviceIdType.MESH
F32 = jnp.float32
BF16 = jnp.bfloat16
HIGHEST = lax.Precision.HIGHEST


def split(x):
    hi = x.astype(BF16)
    lo = (x - hi.astype(F32)).astype(BF16)
    return hi, lo


def kernel(
    tiles, owners, nb, nt, blk, dates, cap, nagg,
    ends_s, count_s, raw_s, rows_s, cols_s, agg_s,
    right_h, diag_h, smooth_h, coup_h,
    ends_v, raw_v, agg_row, cinv,
    out_ref,
    right, stage_d, stage_s, stage_c,
    v, vcat, wsm, wop, part, hot, terms, send, recv,
    bsum, partial_ref, red_in, red_sum, all_in, full, ci, corr_ref,
    ends_row, weight_row, prev_s, last_s, resid, flat, ap3, corr3, send_p, recv_p,
    in_sem, send_sem, recv_sem, psend_sem, precv_sem,
    ra_send, ra_recv, rt_send, rt_recv, rg_send, rg_recv,
    ca_send, ca_recv, ct_send, ct_recv,
):
    t = lax.axis_index("tile")
    g = lax.axis_index("agg")
    slots = 3 * owners * cap
    rows = nagg // owners
    lanes = recv_p.shape[2]

    loads = [
        pltpu.make_async_copy(right_h, right, in_sem.at[0]),
        pltpu.make_async_copy(smooth_h, stage_s, in_sem.at[1]),
        pltpu.make_async_copy(diag_h, stage_d, in_sem.at[2]),
        pltpu.make_async_copy(coup_h, stage_c, in_sem.at[3]),
    ]
    for load in loads:
        load.start()

    def section(i):
        k = i // owners
        h = lax.rem(g + lax.rem(i, owners), owners)
        other = t + k - 1
        valid = (other >= 0) & (other < tiles) & jnp.logical_not((k == 1) & (h == g))
        return k, h, other, valid

    barrier = pltpu.get_barrier_semaphore()

    @pl.loop(0, 3 * owners)
    def _(i):
        k, h, other, valid = section(i)

        @pl.when(valid)
        def _():
            pl.semaphore_signal(barrier, inc=1, device_id=(other, h), device_id_type=MESH)

    @pl.loop(1, tiles)
    def _(d):
        pl.semaphore_signal(
            barrier, inc=1, device_id=(lax.rem(t + d, tiles), g), device_id_type=MESH
        )

    @pl.loop(0, 3 * owners)
    def _(i):
        k, h, other, valid = section(i)

        @pl.when(jnp.logical_not(valid))
        def _():
            for turn in range(recv.shape[0]):
                recv[turn, k * owners + h] = jnp.zeros((cap, dates), F32)
            recv_p[k * owners + h] = jnp.zeros((cap, lanes), F32)

    ci[t * owners + g] = jnp.zeros((1, ci.shape[2]), F32)
    ci[t * owners + g, :, 0:nagg] = cinv[...]

    for k in range(3):
        for h in range(owners):
            at = (k * owners + h) * cap
            ends_row[:, at : at + cap] = ends_v[0, 0, k, h : h + 1, :]
            alive = lax.broadcasted_iota(jnp.int32, (1, cap), 1) < count_s[0, 0, k, h]
            weight_row[:, at : at + cap] = jnp.where(alive, raw_v[0, 0, k, h : h + 1, :], 0.0)

    @pl.loop(0, nt)
    def _(c):
        row = rows_s[c]
        found = row
        for e in range(nt):
            found = jnp.where((rows_s[e] == row) & (e < c), nb + e, found)
        prev_s[c] = found

    @pl.loop(0, nb)
    def _(b):
        found = b
        for e in range(nt):
            found = jnp.where(rows_s[e] == b, nb + e, found)
        last_s[b] = found

    ends = ends_row[...]
    weight = weight_row[...]
    eye = (
        lax.broadcasted_iota(jnp.int32, (blk, blk), 0)
        == lax.broadcasted_iota(jnp.int32, (blk, blk), 1)
    )

    def make_hot(b):
        pick = (lax.broadcasted_iota(jnp.int32, (blk, slots), 0) + b * blk) == ends
        one = jnp.where(pick, 1.0, 0.0).astype(BF16)
        hot[b, :, 0:slots] = one
        hot[b, :, slots : 2 * slots] = one
        return jnp.sum(jnp.where(pick, weight, 0.0), axis=1, keepdims=True)

    def put3(ref, b, x):
        hi, lo = split(x)
        ref[b, 0:blk, :] = hi
        ref[b, blk : 2 * blk, :] = hi
        ref[b, 2 * blk : 3 * blk, :] = lo

    def put3w(ref, b, x):
        hi, lo = split(x)
        ref[b, :, 0:blk] = hi
        ref[b, :, blk : 2 * blk] = lo
        ref[b, :, 2 * blk : 3 * blk] = hi

    def product(w, x):
        return jnp.dot(w, x, preferred_element_type=F32)

    def cat3(x):
        hi, lo = split(x)
        return jnp.concatenate([hi, hi, lo], axis=0)

    loads[0].wait()
    loads[1].wait()

    @pl.loop(0, nb, unroll=2)
    def _(b):
        put3w(wsm, b, stage_s[b])
        new = product(wsm[b], cat3(right[b]))
        v[pl.ds(pl.multiple_of(b * blk, blk), blk), :] = new
        put3(vcat, b, new)

    nvalid = (
        (owners - 1)
        + owners * (t > 0).astype(jnp.int32)
        + owners * (t < tiles - 1).astype(jnp.int32)
    )
    pl.semaphore_wait(barrier, nvalid + tiles - 1)

    def ci_copy_agg(d):
        h = lax.rem(g + d, owners)
        return pltpu.make_async_remote_copy(
            src_ref=ci.at[t * owners + g],
            dst_ref=ci.at[t * owners + g],
            send_sem=ca_send.at[d],
            recv_sem=ca_recv.at[d],
            device_id=(t, h),
            device_id_type=MESH,
        )

    def ci_copy_tile(d):
        return pltpu.make_async_remote_copy(
            src_ref=ci.at[pl.ds(t * owners, owners)],
            dst_ref=ci.at[pl.ds(t * owners, owners)],
            send_sem=ct_send.at[d],
            recv_sem=ct_recv.at[d],
            device_id=(lax.rem(t + d, tiles), g),
            device_id_type=MESH,
        )

    for d in range(1, owners):
        ci_copy_agg(d).start()

    def halo_copy(turn, i):
        k, h, other, valid = section(i)
        return valid, pltpu.make_async_remote_copy(
            src_ref=send.at[turn, i],
            dst_ref=recv.at[turn, (2 - k) * owners + g],
            send_sem=send_sem.at[turn, i],
            recv_sem=recv_sem.at[turn, (2 - k) * owners + g],
            device_id=(other, h),
            device_id_type=MESH,
        )

    def halo_start(turn):
        @pl.loop(0, 3 * owners)
        def _(i):
            k, h, other, valid = section(i)
            count = count_s[0, 0, k, h]
            for s in range(cap):
                end = ends_s[0, 0, k, h, s]
                scale = jnp.where(s < count, raw_s[0, 0, k, h, s], 0.0)
                send[turn, i, s : s + 1, :] = v[pl.ds(end, 1), :] * scale
            _, copy = halo_copy(turn, i)

            @pl.when(valid)
            def _():
                copy.start()

    def basis_copy(i):
        k, h, other, valid = section(i)
        return pltpu.make_async_remote_copy(
            src_ref=send_p.at[i],
            dst_ref=recv_p.at[(2 - k) * owners + g],
            send_sem=psend_sem.at[i],
            recv_sem=precv_sem.at[(2 - k) * owners + g],
            device_id=(other, h),
            device_id_type=MESH,
        )

    def basis_start():
        lane = lax.broadcasted_iota(jnp.int32, (1, lanes), 1)

        @pl.loop(0, 3 * owners)
        def _(i):
            k, h, other, valid = section(i)
            count = count_s[0, 0, k, h]
            for s in range(cap):
                target = agg_s[0, lax.div(ends_s[0, 0, k, h, s], blk)]
                scale = jnp.where(s < count, raw_s[0, 0, k, h, s], 0.0)
                send_p[i, s : s + 1, :] = jnp.where(lane == target, scale, 0.0)

            @pl.when(valid)
            def _():
                basis_copy(i).start()

    def basis_finish():
        @pl.loop(0, 3 * owners)
        def _(i):
            k, h, other, valid = section(i)

            @pl.when(valid)
            def _():
                src = k * owners + h
                pltpu.make_async_remote_copy(
                    src_ref=send_p.at[i],
                    dst_ref=recv_p.at[src],
                    send_sem=psend_sem.at[i],
                    recv_sem=precv_sem.at[src],
                    device_id=(other, h),
                    device_id_type=MESH,
                ).wait()

        lane = lax.broadcasted_iota(jnp.int32, (1, lanes), 1)

        @pl.loop(0, nb, unroll=2)
        def _(b):
            total = jnp.sum(stage_d[b], axis=1, keepdims=True)
            flat[b] = jnp.where(lane == agg_s[0, b], total, 0.0)

        @pl.loop(0, nt, unroll=2)
        def _(c):
            total = jnp.sum(stage_c[c], axis=1, keepdims=True)
            flat[nb + c] = flat[prev_s[c]] + jnp.where(
                lane == agg_s[0, cols_s[c]], total, 0.0
            )

        hi, lo = split(recv_p[...].reshape(slots, lanes))
        heads = jnp.concatenate([hi, lo], axis=0)

        @pl.loop(0, nb // group)
        def _(step):
            arcs = scattered(step * group, heads)
            for i in range(group):
                b = step * group + i
                hi, lo = split(flat[last_s[b]] - arcs[i * blk : (i + 1) * blk])
                ap3[b, :, 0:lanes] = hi
                ap3[b, :, lanes : 2 * lanes] = lo
                ap3[b, :, 2 * lanes : 3 * lanes] = hi

    def halo_finish(turn):
        @pl.loop(0, 3 * owners)
        def _(i):
            k, h, other, valid = section(i)

            @pl.when(valid)
            def _():
                src = k * owners + h
                pltpu.make_async_remote_copy(
                    src_ref=send.at[turn, i],
                    dst_ref=recv.at[turn, src],
                    send_sem=send_sem.at[turn, i],
                    recv_sem=recv_sem.at[turn, src],
                    device_id=(other, h),
                    device_id_type=MESH,
                ).wait()

        @pl.loop(0, 3 * owners)
        def _(i):
            hi, lo = split(recv[turn, i])
            at = pl.multiple_of(i * cap, cap)
            terms[pl.ds(at, cap), :] = hi
            terms[pl.ds(slots + at, cap), :] = lo

    def local_part():
        @pl.loop(0, nb, unroll=8)
        def _(b):
            part[b] = product(wop[b], vcat[b])

        @pl.loop(0, nt, unroll=8)
        def _(c):
            part[nb + c] = part[prev_s[c]] + product(wop[nb + c], vcat[cols_s[c]])

    group = 8 if nb % 8 == 0 else 1

    def scattered(first, source):
        rows_hot = hot[pl.ds(first, group)].reshape(group * blk, 2 * slots)
        return product(rows_hot, source)

    def residuals(first):
        arcs = scattered(first, terms[...])
        return [
            right[first + i] - part[last_s[first + i]] + arcs[i * blk : (i + 1) * blk]
            for i in range(group)
        ]

    def sweep(final):
        @pl.loop(0, nb // group)
        def _(step):
            first = step * group
            rests = residuals(first)
            for i in range(group):
                b = first + i
                at = pl.ds(pl.multiple_of(b * blk, blk), blk)
                new = v[at, :] + product(wsm[b], cat3(rests[i]))
                if final:
                    out_ref[at, :] = new
                else:
                    v[at, :] = new
                    put3(vcat, b, new)

    halo_start(0)
    loads[2].wait()
    loads[3].wait()

    @pl.loop(0, nb)
    def _(b):
        tail = make_hot(b)
        tile = stage_d[b] + jnp.where(eye, tail, 0.0)
        stage_d[b] = tile
        put3w(wop, b, tile)

    @pl.loop(0, nt, unroll=2)
    def _(c):
        put3w(wop, nb + c, stage_c[c])

    local_part()
    for d in range(1, owners):
        ci_copy_agg(d).wait()

    @pl.loop(1, tiles)
    def _(d):
        ci_copy_tile(d).start()

    halo_finish(0)
    sweep(False)

    halo_start(1)
    basis_start()
    local_part()
    halo_finish(1)

    @pl.loop(0, nb // group)
    def _(step):
        rests = residuals(step * group)
        for i in range(group):
            b = step * group + i
            resid[b] = rests[i]
            bsum[pl.ds(b, 1), :] = jnp.sum(rests[i], axis=0, keepdims=True)

    pick_t = jnp.where(
        lax.broadcasted_iota(jnp.int32, (nagg, nb), 0) == agg_row[...], 1.0, 0.0
    )
    partial_ref[...] = jnp.dot(
        pick_t, bsum[...], preferred_element_type=F32, precision=HIGHEST
    )

    def red_copy(d):
        h = lax.rem(g + d, owners)
        return pltpu.make_async_remote_copy(
            src_ref=partial_ref.at[pl.ds(pl.multiple_of(h * rows, rows), rows)],
            dst_ref=red_in.at[d],
            send_sem=ra_send.at[d],
            recv_sem=ra_recv.at[d],
            device_id=(t, h),
            device_id_type=MESH,
        )

    for d in range(1, owners):
        red_copy(d).start()
    basis_finish()
    total = partial_ref[pl.ds(pl.multiple_of(g * rows, rows), rows), :]
    for d in range(1, owners):
        red_copy(d).wait()
        total = total + red_in[d]
    red_sum[...] = total

    def tile_copy(d):
        return pltpu.make_async_remote_copy(
            src_ref=red_sum,
            dst_ref=all_in.at[d],
            send_sem=rt_send.at[d],
            recv_sem=rt_recv.at[d],
            device_id=(lax.rem(t + d, tiles), g),
            device_id_type=MESH,
        )

    @pl.loop(1, tiles)
    def _(d):
        tile_copy(d).start()

    all_in[0] = red_sum[...]

    @pl.loop(1, tiles)
    def _(d):
        tile_copy(d).wait()

    own_rows = pl.ds(pl.multiple_of(g * rows, rows), rows)
    full[own_rows, :] = jnp.sum(all_in[...], axis=0)

    def gather_copy(d):
        h = lax.rem(g + d, owners)
        return pltpu.make_async_remote_copy(
            src_ref=full.at[own_rows],
            dst_ref=full.at[own_rows],
            send_sem=rg_send.at[d],
            recv_sem=rg_recv.at[d],
            device_id=(t, h),
            device_id_type=MESH,
        )

    for d in range(1, owners):
        gather_copy(d).start()

    @pl.loop(1, tiles)
    def _(d):
        ci_copy_tile(d).wait()

    for d in range(1, owners):
        gather_copy(d).wait()

    inverse = ci[...].reshape(nagg, ci.shape[2])[:, 0:nagg]
    corr = jnp.dot(inverse, full[...], preferred_element_type=F32, precision=HIGHEST)
    corr_ref[...] = jnp.zeros_like(corr_ref)
    corr_ref[0:nagg, :] = corr
    corr3[...] = cat3(corr_ref[...])

    @pl.loop(0, nb, unroll=4)
    def _(b):
        at = pl.ds(pl.multiple_of(b * blk, blk), blk)
        rest = resid[b] - product(ap3[b], corr3[...])
        new = v[at, :] + corr_ref[pl.ds(agg_s[0, b], 1), :] + product(wsm[b], cat3(rest))
        v[at, :] = new
        put3(vcat, b, new)

    halo_start(2)
    local_part()
    halo_finish(2)
    sweep(True)


def local(
    tiles, right_side, diag_tiles, smoother, coupling_tiles, tile_rows, tile_cols,
    cross_end, cross_count, cross_weight, block_agg, coarse_inverse,
):
    nb, blk, _ = diag_tiles.shape
    nt = coupling_tiles.shape[0]
    points, dates = right_side.shape
    owners, cap = cross_end.shape[3:]
    nagg = coarse_inverse.shape[1]
    slots = 3 * owners * cap
    rows = nagg // owners
    turns = 3
    lanes = 128 * ((nagg + 127) // 128)

    smem = pl.BlockSpec(memory_space=pltpu.SMEM)
    vmem = pl.BlockSpec(memory_space=pltpu.VMEM)
    hbm = pl.BlockSpec(memory_space=pl.ANY)
    dma = pltpu.SemaphoreType.DMA
    return pl.pallas_call(
        functools.partial(kernel, tiles, owners, nb, nt, blk, dates, cap, nagg),
        out_shape=jax.ShapeDtypeStruct((points, dates), F32),
        in_specs=[smem] * 6 + [hbm] * 4 + [vmem] * 4,
        out_specs=vmem,
        scratch_shapes=[
            pltpu.VMEM((nb, blk, dates), F32),
            pltpu.VMEM((nb, blk, blk), F32),
            pltpu.VMEM((nb, blk, blk), F32),
            pltpu.VMEM((nt, blk, blk), F32),
            pltpu.VMEM((points, dates), F32),
            pltpu.VMEM((nb, 3 * blk, dates), BF16),
            pltpu.VMEM((nb, blk, 3 * blk), BF16),
            pltpu.VMEM((nb + nt, blk, 3 * blk), BF16),
            pltpu.VMEM((nb + nt, blk, dates), F32),
            pltpu.VMEM((nb, blk, 2 * slots), BF16),
            pltpu.VMEM((2 * slots, dates), BF16),
            pltpu.VMEM((turns, 3 * owners, cap, dates), F32),
            pltpu.VMEM((turns, 3 * owners, cap, dates), F32),
            pltpu.VMEM((nb, dates), F32),
            pltpu.VMEM((nagg, dates), F32),
            pltpu.VMEM((owners, rows, dates), F32),
            pltpu.VMEM((rows, dates), F32),
            pltpu.VMEM((tiles, rows, dates), F32),
            pltpu.VMEM((nagg, dates), F32),
            pltpu.VMEM((nagg, 1, lanes), F32),
            pltpu.VMEM((lanes, dates), F32),
            pltpu.VMEM((1, slots), jnp.int32),
            pltpu.VMEM((1, slots), F32),
            pltpu.SMEM((nt,), jnp.int32),
            pltpu.SMEM((nb,), jnp.int32),
            pltpu.VMEM((nb, blk, dates), F32),
            pltpu.VMEM((nb + nt, blk, lanes), F32),
            pltpu.VMEM((nb, blk, 3 * lanes), BF16),
            pltpu.VMEM((3 * lanes, dates), BF16),
            pltpu.VMEM((3 * owners, cap, lanes), F32),
            pltpu.VMEM((3 * owners, cap, lanes), F32),
            dma((4,)),
            dma((turns, 3 * owners)),
            dma((turns, 3 * owners)),
            dma((3 * owners,)),
            dma((3 * owners,)),
            dma((owners,)), dma((owners,)),
            dma((tiles,)), dma((tiles,)),
            dma((owners,)), dma((owners,)),
            dma((owners,)), dma((owners,)),
            dma((tiles,)), dma((tiles,)),
        ],
        compiler_params=pltpu.CompilerParams(
            collective_id=0, has_side_effects=True, vmem_limit_bytes=56 * 1024 * 1024
        ),
        cost_estimate=pl.CostEstimate(
            flops=8 * 256 * blk * blk * dates, bytes_accessed=8 << 20, transcendentals=0
        ),
    )(
        cross_end, cross_count, cross_weight, tile_rows, tile_cols, block_agg.reshape(1, nb),
        right_side.reshape(nb, blk, dates), diag_tiles, smoother, coupling_tiles,
        cross_end, cross_weight, block_agg.reshape(1, nb), coarse_inverse,
    )


def solution(mesh):
    both = ("tile", "agg")
    placed = (
        P(both, None),
        P(both, None, None),
        P(both, None, None),
        P(both, None, None),
        P(both),
        P(both),
        P("tile", "agg", None, None, None),
        P("tile", "agg", None, None),
        P("tile", "agg", None, None, None),
        P(both, None),
        P(both, None),
    )
    return jax.shard_map(
        functools.partial(local, mesh.shape["tile"]),
        mesh=mesh, in_specs=placed, out_specs=P(both, None), check_vma=False,
    )
```

```python
import functools

import jax
import jax.numpy as jnp
from jax import lax
from jax.experimental import pallas as pl
from jax.experimental.pallas import tpu as pltpu
from jax.sharding import PartitionSpec as P

MESH = pl.DeviceIdType.MESH
F32 = jnp.float32
BF16 = jnp.bfloat16
HIGHEST = lax.Precision.HIGHEST


def split(x):
    hi = x.astype(BF16)
    lo = (x - hi.astype(F32)).astype(BF16)
    return hi, lo


def kernel(
    tiles, owners, nb, nt, blk, dates, cap, nagg,
    ends_s, count_s, raw_s, rows_s, cols_s, agg_s,
    right_h, diag_h, smooth_h, coup_h,
    ends_v, raw_v, agg_row, cinv,
    out_ref,
    right, stage_d, stage_s, stage_c,
    v, vcat, wsm, wop, part, hot, terms, send, recv,
    bsum, partial_ref, red_in, red_sum, all_in, full, ci, corr_ref,
    ends_row, weight_row, prev_s, last_s, resid, flat, ap3, corr3, send_p, recv_p,
    in_sem, send_sem, recv_sem, psend_sem, precv_sem,
    ra_send, ra_recv, rt_send, rt_recv, rg_send, rg_recv,
    ca_send, ca_recv, ct_send, ct_recv,
):
    t = lax.axis_index("tile")
    g = lax.axis_index("agg")
    slots = 3 * owners * cap
    rows = nagg // owners
    lanes = recv_p.shape[2]

    loads = [
        pltpu.make_async_copy(right_h, right, in_sem.at[0]),
        pltpu.make_async_copy(smooth_h, stage_s, in_sem.at[1]),
        pltpu.make_async_copy(diag_h, stage_d, in_sem.at[2]),
        pltpu.make_async_copy(coup_h, stage_c, in_sem.at[3]),
    ]
    for load in loads:
        load.start()

    def section(i):
        k = i // owners
        h = lax.rem(g + lax.rem(i, owners), owners)
        other = t + k - 1
        valid = (other >= 0) & (other < tiles) & jnp.logical_not((k == 1) & (h == g))
        return k, h, other, valid

    barrier = pltpu.get_barrier_semaphore()

    @pl.loop(0, 3 * owners)
    def _(i):
        k, h, other, valid = section(i)

        @pl.when(valid)
        def _():
            pl.semaphore_signal(barrier, inc=1, device_id=(other, h), device_id_type=MESH)

    @pl.loop(1, tiles)
    def _(d):
        pl.semaphore_signal(
            barrier, inc=1, device_id=(lax.rem(t + d, tiles), g), device_id_type=MESH
        )

    @pl.loop(0, 3 * owners)
    def _(i):
        k, h, other, valid = section(i)

        @pl.when(jnp.logical_not(valid))
        def _():
            for turn in range(recv.shape[0]):
                recv[turn, k * owners + h] = jnp.zeros((cap, dates), F32)
            recv_p[k * owners + h] = jnp.zeros((cap, lanes), F32)

    ci[t * owners + g] = jnp.zeros((1, ci.shape[2]), F32)
    ci[t * owners + g, :, 0:nagg] = cinv[...]

    for k in range(3):
        for h in range(owners):
            at = (k * owners + h) * cap
            ends_row[:, at : at + cap] = ends_v[0, 0, k, h : h + 1, :]
            alive = lax.broadcasted_iota(jnp.int32, (1, cap), 1) < count_s[0, 0, k, h]
            weight_row[:, at : at + cap] = jnp.where(alive, raw_v[0, 0, k, h : h + 1, :], 0.0)

    @pl.loop(0, nt)
    def _(c):
        row = rows_s[c]
        found = row
        for e in range(nt):
            found = jnp.where((rows_s[e] == row) & (e < c), nb + e, found)
        prev_s[c] = found

    @pl.loop(0, nb)
    def _(b):
        found = b
        for e in range(nt):
            found = jnp.where(rows_s[e] == b, nb + e, found)
        last_s[b] = found

    ends = ends_row[...]
    weight = weight_row[...]
    eye = (
        lax.broadcasted_iota(jnp.int32, (blk, blk), 0)
        == lax.broadcasted_iota(jnp.int32, (blk, blk), 1)
    )

    def make_hot(b):
        pick = (lax.broadcasted_iota(jnp.int32, (blk, slots), 0) + b * blk) == ends
        one = jnp.where(pick, 1.0, 0.0).astype(BF16)
        hot[b, :, 0:slots] = one
        hot[b, :, slots : 2 * slots] = one
        return jnp.sum(jnp.where(pick, weight, 0.0), axis=1, keepdims=True)

    def put3(ref, b, x):
        hi, lo = split(x)
        ref[b, 0:blk, :] = hi
        ref[b, blk : 2 * blk, :] = hi
        ref[b, 2 * blk : 3 * blk, :] = lo

    def put3w(ref, b, x):
        hi, lo = split(x)
        ref[b, :, 0:blk] = hi
        ref[b, :, blk : 2 * blk] = lo
        ref[b, :, 2 * blk : 3 * blk] = hi

    def product(w, x):
        return jnp.dot(w, x, preferred_element_type=F32)

    def cat3(x):
        hi, lo = split(x)
        return jnp.concatenate([hi, hi, lo], axis=0)

    loads[0].wait()
    loads[1].wait()

    @pl.loop(0, nb, unroll=8)
    def _(b):
        put3w(wsm, b, stage_s[b])
        new = product(wsm[b], cat3(right[b]))
        v[pl.ds(pl.multiple_of(b * blk, blk), blk), :] = new
        put3(vcat, b, new)

    nvalid = (
        (owners - 1)
        + owners * (t > 0).astype(jnp.int32)
        + owners * (t < tiles - 1).astype(jnp.int32)
    )
    pl.semaphore_wait(barrier, nvalid + tiles - 1)

    def ci_copy_agg(d):
        h = lax.rem(g + d, owners)
        return pltpu.make_async_remote_copy(
            src_ref=ci.at[t * owners + g],
            dst_ref=ci.at[t * owners + g],
            send_sem=ca_send.at[d],
            recv_sem=ca_recv.at[d],
            device_id=(t, h),
            device_id_type=MESH,
        )

    def ci_copy_tile(d):
        return pltpu.make_async_remote_copy(
            src_ref=ci.at[pl.ds(t * owners, owners)],
            dst_ref=ci.at[pl.ds(t * owners, owners)],
            send_sem=ct_send.at[d],
            recv_sem=ct_recv.at[d],
            device_id=(lax.rem(t + d, tiles), g),
            device_id_type=MESH,
        )

    for d in range(1, owners):
        ci_copy_agg(d).start()

    def halo_copy(turn, i):
        k, h, other, valid = section(i)
        return valid, pltpu.make_async_remote_copy(
            src_ref=send.at[turn, i],
            dst_ref=recv.at[turn, (2 - k) * owners + g],
            send_sem=send_sem.at[turn, i],
            recv_sem=recv_sem.at[turn, (2 - k) * owners + g],
            device_id=(other, h),
            device_id_type=MESH,
        )

    def halo_start(turn):
        @pl.loop(0, 3 * owners)
        def _(i):
            k, h, other, valid = section(i)
            count = count_s[0, 0, k, h]
            for s in range(cap):
                end = ends_s[0, 0, k, h, s]
                scale = jnp.where(s < count, raw_s[0, 0, k, h, s], 0.0)
                send[turn, i, s : s + 1, :] = v[pl.ds(end, 1), :] * scale
            _, copy = halo_copy(turn, i)

            @pl.when(valid)
            def _():
                copy.start()

    def basis_copy(i):
        k, h, other, valid = section(i)
        return pltpu.make_async_remote_copy(
            src_ref=send_p.at[i],
            dst_ref=recv_p.at[(2 - k) * owners + g],
            send_sem=psend_sem.at[i],
            recv_sem=precv_sem.at[(2 - k) * owners + g],
            device_id=(other, h),
            device_id_type=MESH,
        )

    def basis_start():
        lane = lax.broadcasted_iota(jnp.int32, (1, lanes), 1)

        @pl.loop(0, 3 * owners)
        def _(i):
            k, h, other, valid = section(i)
            count = count_s[0, 0, k, h]
            for s in range(cap):
                target = agg_s[0, lax.div(ends_s[0, 0, k, h, s], blk)]
                scale = jnp.where(s < count, raw_s[0, 0, k, h, s], 0.0)
                send_p[i, s : s + 1, :] = jnp.where(lane == target, scale, 0.0)

            @pl.when(valid)
            def _():
                basis_copy(i).start()

    def basis_finish():
        @pl.loop(0, 3 * owners)
        def _(i):
            k, h, other, valid = section(i)

            @pl.when(valid)
            def _():
                src = k * owners + h
                pltpu.make_async_remote_copy(
                    src_ref=send_p.at[i],
                    dst_ref=recv_p.at[src],
                    send_sem=psend_sem.at[i],
                    recv_sem=precv_sem.at[src],
                    device_id=(other, h),
                    device_id_type=MESH,
                ).wait()

        lane = lax.broadcasted_iota(jnp.int32, (1, lanes), 1)

        @pl.loop(0, nb, unroll=2)
        def _(b):
            total = jnp.sum(stage_d[b], axis=1, keepdims=True)
            flat[b] = jnp.where(lane == agg_s[0, b], total, 0.0)

        @pl.loop(0, nt, unroll=2)
        def _(c):
            total = jnp.sum(stage_c[c], axis=1, keepdims=True)
            flat[nb + c] = flat[prev_s[c]] + jnp.where(
                lane == agg_s[0, cols_s[c]], total, 0.0
            )

        hi, lo = split(recv_p[...].reshape(slots, lanes))
        heads = jnp.concatenate([hi, lo], axis=0)

        @pl.loop(0, nb // group)
        def _(step):
            arcs = scattered(step * group, heads)
            for i in range(group):
                b = step * group + i
                hi, lo = split(flat[last_s[b]] - arcs[i * blk : (i + 1) * blk])
                ap3[b, :, 0:lanes] = hi
                ap3[b, :, lanes : 2 * lanes] = lo
                ap3[b, :, 2 * lanes : 3 * lanes] = hi

    def halo_finish(turn):
        @pl.loop(0, 3 * owners)
        def _(i):
            k, h, other, valid = section(i)

            @pl.when(valid)
            def _():
                src = k * owners + h
                pltpu.make_async_remote_copy(
                    src_ref=send.at[turn, i],
                    dst_ref=recv.at[turn, src],
                    send_sem=send_sem.at[turn, i],
                    recv_sem=recv_sem.at[turn, src],
                    device_id=(other, h),
                    device_id_type=MESH,
                ).wait()

        @pl.loop(0, 3 * owners)
        def _(i):
            hi, lo = split(recv[turn, i])
            at = pl.multiple_of(i * cap, cap)
            terms[pl.ds(at, cap), :] = hi
            terms[pl.ds(slots + at, cap), :] = lo

    def local_part():
        @pl.loop(0, nb, unroll=16)
        def _(b):
            part[b] = product(wop[b], vcat[b])

        @pl.loop(0, nt, unroll=16)
        def _(c):
            part[nb + c] = part[prev_s[c]] + product(wop[nb + c], vcat[cols_s[c]])

    group = 8 if nb % 8 == 0 else 1

    def scattered(first, source):
        rows_hot = hot[pl.ds(first, group)].reshape(group * blk, 2 * slots)
        return product(rows_hot, source)

    def residuals(first):
        arcs = scattered(first, terms[...])
        return [
            right[first + i] - part[last_s[first + i]] + arcs[i * blk : (i + 1) * blk]
            for i in range(group)
        ]

    def sweep(final):
        @pl.loop(0, nb // group)
        def _(step):
            first = step * group
            rests = residuals(first)
            for i in range(group):
                b = first + i
                at = pl.ds(pl.multiple_of(b * blk, blk), blk)
                new = v[at, :] + product(wsm[b], cat3(rests[i]))
                if final:
                    out_ref[at, :] = new
                else:
                    v[at, :] = new
                    put3(vcat, b, new)

    halo_start(0)
    loads[2].wait()
    loads[3].wait()

    @pl.loop(0, nb, unroll=2)
    def _(b):
        tail = make_hot(b)
        tile = stage_d[b] + jnp.where(eye, tail, 0.0)
        stage_d[b] = tile
        put3w(wop, b, tile)

    @pl.loop(0, nt, unroll=2)
    def _(c):
        put3w(wop, nb + c, stage_c[c])

    local_part()
    for d in range(1, owners):
        ci_copy_agg(d).wait()

    @pl.loop(1, tiles)
    def _(d):
        ci_copy_tile(d).start()

    halo_finish(0)
    sweep(False)

    halo_start(1)
    basis_start()
    local_part()
    halo_finish(1)

    @pl.loop(0, nb // group)
    def _(step):
        rests = residuals(step * group)
        for i in range(group):
            b = step * group + i
            resid[b] = rests[i]
            bsum[pl.ds(b, 1), :] = jnp.sum(rests[i], axis=0, keepdims=True)

    pick_t = jnp.where(
        lax.broadcasted_iota(jnp.int32, (nagg, nb), 0) == agg_row[...], 1.0, 0.0
    )
    partial_ref[...] = jnp.dot(
        pick_t, bsum[...], preferred_element_type=F32, precision=HIGHEST
    )

    def red_copy(d):
        h = lax.rem(g + d, owners)
        return pltpu.make_async_remote_copy(
            src_ref=partial_ref.at[pl.ds(pl.multiple_of(h * rows, rows), rows)],
            dst_ref=red_in.at[d],
            send_sem=ra_send.at[d],
            recv_sem=ra_recv.at[d],
            device_id=(t, h),
            device_id_type=MESH,
        )

    for d in range(1, owners):
        red_copy(d).start()
    basis_finish()
    total = partial_ref[pl.ds(pl.multiple_of(g * rows, rows), rows), :]
    for d in range(1, owners):
        red_copy(d).wait()
        total = total + red_in[d]
    red_sum[...] = total

    def tile_copy(d):
        return pltpu.make_async_remote_copy(
            src_ref=red_sum,
            dst_ref=all_in.at[d],
            send_sem=rt_send.at[d],
            recv_sem=rt_recv.at[d],
            device_id=(lax.rem(t + d, tiles), g),
            device_id_type=MESH,
        )

    @pl.loop(1, tiles)
    def _(d):
        tile_copy(d).start()

    all_in[0] = red_sum[...]

    @pl.loop(1, tiles)
    def _(d):
        tile_copy(d).wait()

    own_rows = pl.ds(pl.multiple_of(g * rows, rows), rows)
    full[own_rows, :] = jnp.sum(all_in[...], axis=0)

    def gather_copy(d):
        h = lax.rem(g + d, owners)
        return pltpu.make_async_remote_copy(
            src_ref=full.at[own_rows],
            dst_ref=full.at[own_rows],
            send_sem=rg_send.at[d],
            recv_sem=rg_recv.at[d],
            device_id=(t, h),
            device_id_type=MESH,
        )

    for d in range(1, owners):
        gather_copy(d).start()

    @pl.loop(1, tiles)
    def _(d):
        ci_copy_tile(d).wait()

    for d in range(1, owners):
        gather_copy(d).wait()

    inverse = ci[...].reshape(nagg, ci.shape[2])[:, 0:nagg]
    corr = jnp.dot(inverse, full[...], preferred_element_type=F32, precision=HIGHEST)
    corr_ref[...] = jnp.zeros_like(corr_ref)
    corr_ref[0:nagg, :] = corr
    corr3[...] = cat3(corr_ref[...])

    @pl.loop(0, nb, unroll=8)
    def _(b):
        at = pl.ds(pl.multiple_of(b * blk, blk), blk)
        rest = resid[b] - product(ap3[b], corr3[...])
        new = v[at, :] + corr_ref[pl.ds(agg_s[0, b], 1), :] + product(wsm[b], cat3(rest))
        v[at, :] = new
        put3(vcat, b, new)

    halo_start(2)
    local_part()
    halo_finish(2)
    sweep(True)


def local(
    tiles, right_side, diag_tiles, smoother, coupling_tiles, tile_rows, tile_cols,
    cross_end, cross_count, cross_weight, block_agg, coarse_inverse,
):
    nb, blk, _ = diag_tiles.shape
    nt = coupling_tiles.shape[0]
    points, dates = right_side.shape
    owners, cap = cross_end.shape[3:]
    nagg = coarse_inverse.shape[1]
    slots = 3 * owners * cap
    rows = nagg // owners
    turns = 3
    lanes = 128 * ((nagg + 127) // 128)

    smem = pl.BlockSpec(memory_space=pltpu.SMEM)
    vmem = pl.BlockSpec(memory_space=pltpu.VMEM)
    hbm = pl.BlockSpec(memory_space=pl.ANY)
    dma = pltpu.SemaphoreType.DMA
    return pl.pallas_call(
        functools.partial(kernel, tiles, owners, nb, nt, blk, dates, cap, nagg),
        out_shape=jax.ShapeDtypeStruct((points, dates), F32),
        in_specs=[smem] * 6 + [hbm] * 4 + [vmem] * 4,
        out_specs=vmem,
        scratch_shapes=[
            pltpu.VMEM((nb, blk, dates), F32),
            pltpu.VMEM((nb, blk, blk), F32),
            pltpu.VMEM((nb, blk, blk), F32),
            pltpu.VMEM((nt, blk, blk), F32),
            pltpu.VMEM((points, dates), F32),
            pltpu.VMEM((nb, 3 * blk, dates), BF16),
            pltpu.VMEM((nb, blk, 3 * blk), BF16),
            pltpu.VMEM((nb + nt, blk, 3 * blk), BF16),
            pltpu.VMEM((nb + nt, blk, dates), F32),
            pltpu.VMEM((nb, blk, 2 * slots), BF16),
            pltpu.VMEM((2 * slots, dates), BF16),
            pltpu.VMEM((turns, 3 * owners, cap, dates), F32),
            pltpu.VMEM((turns, 3 * owners, cap, dates), F32),
            pltpu.VMEM((nb, dates), F32),
            pltpu.VMEM((nagg, dates), F32),
            pltpu.VMEM((owners, rows, dates), F32),
            pltpu.VMEM((rows, dates), F32),
            pltpu.VMEM((tiles, rows, dates), F32),
            pltpu.VMEM((nagg, dates), F32),
            pltpu.VMEM((nagg, 1, lanes), F32),
            pltpu.VMEM((lanes, dates), F32),
            pltpu.VMEM((1, slots), jnp.int32),
            pltpu.VMEM((1, slots), F32),
            pltpu.SMEM((nt,), jnp.int32),
            pltpu.SMEM((nb,), jnp.int32),
            pltpu.VMEM((nb, blk, dates), F32),
            pltpu.VMEM((nb + nt, blk, lanes), F32),
            pltpu.VMEM((nb, blk, 3 * lanes), BF16),
            pltpu.VMEM((3 * lanes, dates), BF16),
            pltpu.VMEM((3 * owners, cap, lanes), F32),
            pltpu.VMEM((3 * owners, cap, lanes), F32),
            dma((4,)),
            dma((turns, 3 * owners)),
            dma((turns, 3 * owners)),
            dma((3 * owners,)),
            dma((3 * owners,)),
            dma((owners,)), dma((owners,)),
            dma((tiles,)), dma((tiles,)),
            dma((owners,)), dma((owners,)),
            dma((owners,)), dma((owners,)),
            dma((tiles,)), dma((tiles,)),
        ],
        compiler_params=pltpu.CompilerParams(
            collective_id=0, has_side_effects=True, vmem_limit_bytes=56 * 1024 * 1024
        ),
        cost_estimate=pl.CostEstimate(
            flops=8 * 256 * blk * blk * dates, bytes_accessed=8 << 20, transcendentals=0
        ),
    )(
        cross_end, cross_count, cross_weight, tile_rows, tile_cols, block_agg.reshape(1, nb),
        right_side.reshape(nb, blk, dates), diag_tiles, smoother, coupling_tiles,
        cross_end, cross_weight, block_agg.reshape(1, nb), coarse_inverse,
    )


def solution(mesh):
    both = ("tile", "agg")
    placed = (
        P(both, None),
        P(both, None, None),
        P(both, None, None),
        P(both, None, None),
        P(both),
        P(both),
        P("tile", "agg", None, None, None),
        P("tile", "agg", None, None),
        P("tile", "agg", None, None, None),
        P(both, None),
        P(both, None),
    )
    return jax.shard_map(
        functools.partial(local, mesh.shape["tile"]),
        mesh=mesh, in_specs=placed, out_specs=P(both, None), check_vma=False,
    )
```
